32 devices in a mesh: dp: 2 (over core), glob: 4 (over y, x), byte: 4 (over z).
Axes of the slice: x: 2, y: 2, z: 4, core: 2. Of those that a mesh axis runs over, the one named last changes fastest.
Arguments:
- byte_states: bfloat16 [2, 512, 4096], P('dp', 'byte', 'glob'), may hold values from -8 to 8
- patch_start: int32 [2, 4, 32], P('dp'), may hold values from 0 to 128, as said below
- queries: bfloat16 [2, 128, 2048], P('dp', 'byte', 'glob'), may hold values from -6 to 6
- grad_out: bfloat16 [2, 128, 2048], P('dp', 'byte', 'glob'), may hold values from -6 to 6
- w_kv: bfloat16 [2, 4096, 512], P(None, 'byte', 'glob'), may hold values from -0.09375 to 0.09375
Outputs:
- attended: bfloat16 [2, 128, 2048], P('dp', 'byte', 'glob')
- grad_queries: bfloat16 [2, 128, 2048], P('dp', 'byte', 'glob')
- grad_bytes: bfloat16 [2, 512, 4096], P('dp', 'byte', 'glob')
- grad_kv: float32 [2, 4096, 512], P(None, 'byte', 'glob')
The draws below stay inside these ranges and needn't reach their ends.
Inputs may be any that keep to these rules, and one draw needn't show every extreme that they name: Per shard: patch_start[s, 0] is 0, used slots come first with strictly rising starts, unused slots hold 128; a shard uses between 8 and 32 slots, and some shard of every draw uses all 32.
All inputs are finite; a program needn't handle non-finite values.
Results may differ from the reference program's by a relative error of at most 0.02.
Values may be sent and summed in bfloat16 or wider, within the bound.
A program may use at most 64 MiB of HBM per device.

```python
import math
import jax
import jax.numpy as jnp
from jax import lax

D = 4096
HS = 128
HQ = 16
HK = 4
BYTE_DEV = 128
PMAX = 32
SEQS = 2
BYTES = 512
SLOTS = 128
N_BYTE = 4


def draw_byte_states(key, part):
    base = jax.random.normal(jax.random.fold_in(key, 11), (SEQS, BYTES, D), jnp.float32)
    base = jnp.clip(base, -8.0, 8.0)
    return base.astype(jnp.bfloat16)


def draw_patch_start(key, part):
    row_total = SEQS * N_BYTE
    first_key = jax.random.fold_in(key, 21)
    second_key = jax.random.fold_in(key, 22)
    third_key = jax.random.fold_in(key, 23)
    fourth_key = jax.random.fold_in(key, 24)
    drawn = jax.random.randint(first_key, (row_total,), PMAX // 4, 3 * PMAX // 4 + 1)
    filled = jax.random.randint(second_key, (row_total,), 0, 8) == 0
    forced = jax.random.randint(third_key, (), 0, row_total)
    filled = filled | (jnp.arange(row_total) == forced)
    used = jnp.where(filled, PMAX, drawn)
    scores = jax.random.randint(fourth_key, (row_total, BYTE_DEV - 1), 0, 1 << 16) * BYTE_DEV + jnp.arange(BYTE_DEV - 1)[None, :]
    unused, chosen = lax.top_k(scores, PMAX - 1)
    chosen = chosen + 1
    place = jnp.arange(PMAX - 1)[None, :]
    chosen = jnp.where(place < used[:, None] - 1, chosen, BYTE_DEV)
    chosen = jnp.sort(chosen, axis=1)
    starts = jnp.concatenate([jnp.zeros((row_total, 1), jnp.int32), chosen.astype(jnp.int32)], axis=1)
    return starts.reshape(SEQS, N_BYTE, PMAX)


def level_of(rng, shape, split, smallest, largest):
    def one(axis_at, shards_of):
        heights = jax.random.uniform(jax.random.fold_in(jax.random.fold_in(rng, 6), axis_at), (shards_of,), jnp.float32, smallest / len(split), largest / len(split))
        return jnp.repeat(jnp.exp(heights), shape[axis_at] // shards_of).reshape((-1,) + (1,) * (len(shape) - axis_at - 1))

    gain = one(*split[0])
    for cut in split[1:]:
        gain = gain * one(*cut)
    return gain


def centred(rng, dims, width, reach, shards=(), held_as=jnp.bfloat16):
    values = jax.random.normal(rng, dims, jnp.float32) * width
    if len(shards) > 0:
        values = level_of(rng, dims, shards, -0.22, 0.18) * values
    return jnp.clip(values, min=-reach, max=reach).astype(held_as)


def setup_inputs(seed: int = 0) -> dict:
    keys = jax.random.split(jax.random.key(seed), 6)
    return {
        "byte_states": draw_byte_states(jax.random.fold_in(keys[5], 71), 0),
        "patch_start": draw_patch_start(jax.random.fold_in(keys[5], 71), 0),
        "queries": centred(keys[2], (SEQS, SLOTS, HQ * HS), 1.0, 6.0, ((0, 2), (1, 4), (2, 4))),
        "grad_out": centred(keys[3], (SEQS, SLOTS, HQ * HS), 1.0, 6.0, ((0, 2), (1, 4), (2, 4))),
        "w_kv": centred(keys[4], (2, D, HK * HS), D ** -0.5, 0.09375, ((1, 4), (2, 4))),
    }


def segment_of(offsets, length):
    position = jnp.arange(length, dtype=jnp.int32)
    opened = (offsets[:, None] <= position[None, :]).astype(jnp.int32)
    return lax.optimization_barrier(jnp.sum(opened, axis=0)) - 1

def rounded(values_in):
    return lax.optimization_barrier(values_in.astype(jnp.bfloat16)).astype(jnp.float32)

def contract_rows(left, right):
    return lax.dot_general(left, right, (((0,), (0,)), ((), ())), preferred_element_type=jnp.float32)

def reference(byte_states, patch_start, queries, grad_out, w_kv):
    factor = 1.0 / math.sqrt(HS)
    group_size = HQ // HK
    slot_total = N_BYTE * PMAX
    key_ids = jnp.arange(slot_total, dtype=jnp.int32)
    slot_range = jnp.arange(PMAX, dtype=jnp.int32)
    shard_range = jnp.arange(N_BYTE, dtype=jnp.int32)
    grad_pair = jnp.zeros((D, 2 * HK * HS), jnp.float32)
    attended = []
    query_grads_all = []
    byte_grads = []
    for sequence in range(SEQS):
        states = byte_states[sequence].reshape(N_BYTE, BYTE_DEV, D)
        offsets = patch_start[sequence]
        segments = jax.vmap(lambda offset_row: segment_of(offset_row, BYTE_DEV))(offsets)
        members = (slot_range[None, :, None] == segments[:, None, :]).astype(jnp.float32)
        counts = jnp.maximum(lax.optimization_barrier(jnp.sum(members, axis=2)), 1.0)
        summed = jnp.einsum('spb,sbc->spc', members, states.astype(jnp.float32))
        pooled = (summed / counts[:, :, None]).astype(jnp.bfloat16).reshape(slot_total, D)
        usable = (offsets < BYTE_DEV).reshape(slot_total)
        seq_queries = queries[sequence]
        key_rows = jnp.dot(pooled, w_kv[0], preferred_element_type=jnp.float32).astype(jnp.bfloat16)
        value_rows = jnp.dot(pooled, w_kv[1], preferred_element_type=jnp.float32).astype(jnp.bfloat16)
        key_heads = key_rows.astype(jnp.float32).reshape(slot_total, HK, HS)
        value_heads = value_rows.astype(jnp.float32).reshape(slot_total, HK, HS)
        cotangent = grad_out[sequence]

        def per_shard(carried, shard_index):
            key_sum, value_sum = carried
            first = shard_index * PMAX
            local_query = lax.dynamic_slice_in_dim(seq_queries, first, PMAX, 0).astype(jnp.float32).reshape(PMAX, HK, group_size, HS)
            local_grad = lax.dynamic_slice_in_dim(cotangent, first, PMAX, 0).astype(jnp.float32).reshape(PMAX, HK, group_size, HS)
            live = lax.dynamic_slice_in_dim(usable, first, PMAX, 0).astype(jnp.float32)[:, None, None, None]
            query_ids = first + slot_range
            visible = (key_ids[None, :] <= query_ids[:, None]) & usable[None, :]
            scores = jnp.einsum('qcgd,kcd->cgqk', local_query, key_heads) * factor
            masked = jnp.where(visible, scores, -1e+30)
            highest = lax.optimization_barrier(jnp.max(masked, axis=-1, keepdims=True))
            raised = jnp.where(visible, jnp.exp(masked - highest), 0.0)
            totals = jnp.maximum(lax.optimization_barrier(jnp.sum(raised, axis=-1, keepdims=True)), 1.0)
            attention = raised / totals
            shortened = rounded(attention)
            mixed = jnp.einsum('cgqk,kcd->qcgd', shortened, value_heads)
            outputs = (mixed * live).astype(jnp.bfloat16).reshape(PMAX, HQ * HS)
            masked_grad = local_grad * live
            row_dots = jnp.einsum('qcgd,qcgd->cgq', masked_grad, mixed)
            prob_grad = jnp.einsum('qcgd,kcd->cgqk', masked_grad, value_heads)
            score_grad = rounded(attention * (prob_grad - row_dots[..., None]) * factor)
            query_grad = jnp.einsum('cgqk,kcd->qcgd', score_grad, key_heads).astype(jnp.bfloat16).reshape(PMAX, HQ * HS)
            key_part = jnp.einsum('cgqk,qcgd->kcd', score_grad, local_query).reshape(slot_total, HK * HS)
            value_part = jnp.einsum('cgqk,qcgd->kcd', shortened, masked_grad).reshape(slot_total, HK * HS)
            return ((key_sum + rounded(key_part), value_sum + rounded(value_part)), (outputs, query_grad))
        zero_keys = jnp.zeros((slot_total, HK * HS), jnp.float32)
        (key_sum, value_sum), (outputs, query_grads) = lax.scan(per_shard, (zero_keys, zero_keys), shard_range)
        attended.append(outputs.reshape(slot_total, HQ * HS))
        query_grads_all.append(query_grads.reshape(slot_total, HQ * HS))
        key_grad = key_sum.astype(jnp.bfloat16)
        value_grad = value_sum.astype(jnp.bfloat16)
        patch_grad = (jnp.dot(key_grad, w_kv[0].T, preferred_element_type=jnp.float32) + jnp.dot(value_grad, w_kv[1].T, preferred_element_type=jnp.float32)).astype(jnp.bfloat16)
        pool_grad = patch_grad.astype(jnp.float32) / counts.reshape(slot_total)[:, None]
        picked = (shard_range[:, None] * PMAX + segments).reshape(BYTES).astype(jnp.int32)
        byte_grads.append(jnp.take(pool_grad, picked, axis=0).astype(jnp.bfloat16))
        key_value = jnp.concatenate([key_grad, value_grad], axis=1)

        def weight_terms(pair_sum, shard_index):
            first = shard_index * PMAX
            pooled_piece = lax.dynamic_slice_in_dim(pooled, first, PMAX, 0)
            pair_piece = lax.dynamic_slice_in_dim(key_value, first, PMAX, 0)
            return (pair_sum + rounded(contract_rows(pooled_piece, pair_piece)), None)
        pair_add, unused = lax.scan(weight_terms, jnp.zeros((D, 2 * HK * HS), jnp.float32), shard_range)
        grad_pair = grad_pair + pair_add
    grad_kv = grad_pair.reshape(D, 2, HK * HS).transpose(1, 0, 2)
    return (jnp.stack(attended), jnp.stack(query_grads_all), jnp.stack(byte_grads), grad_kv)
```

```python
import functools
import math

import jax
import jax.numpy as jnp
from jax import lax
from jax.experimental import pallas as pl
from jax.experimental.pallas import tpu as pltpu
from jax.sharding import PartitionSpec as P

HS = 128
MESH = pl.DeviceIdType.MESH
F32 = jnp.float32
BF16 = jnp.bfloat16


def mm(left, right, a, b):
    return lax.dot_general(left, right, (((a,), (b,)), ((), ())), preferred_element_type=F32)


def kernel(nd, ng, nb, states_ref, start_ref, query_ref, cot_ref, w_ref,
           att_ref, gq_ref, gb_ref, gkv_ref,
           pooled, pool_all, kv_part, kv_recv, kv_all, dkv_part, dkv_recv, dkv_all, dpart, drecv,
           s1, r1, s2, r2, s3, r3, s4, r4, s5, r5, s6, r6, sd, rd):
    dp = lax.axis_index("dp")
    g = lax.axis_index("glob")
    b = lax.axis_index("byte")
    ratio = nb // ng
    owner = b // ratio
    piece = lax.rem(b, ratio)
    diagonal = g == owner
    byte_count = states_ref.shape[1]
    slots = start_ref.shape[2]
    total = nb * slots
    chunk = w_ref.shape[1]
    width = w_ref.shape[2]
    shared = width // HS
    group = query_ref.shape[2] // width
    factor = 1.0 / math.sqrt(HS)

    def remote(src, dst, send, recv, **where):
        return pltpu.make_async_remote_copy(
            src_ref=src, dst_ref=dst, send_sem=send, recv_sem=recv,
            device_id=where, device_id_type=MESH)

    def unless(cond, fn):
        pl.when(jnp.logical_not(cond))(fn)

    barrier = pltpu.get_barrier_semaphore()

    def greet(**where):
        pl.semaphore_signal(barrier, inc=1, device_id=where, device_id_type=MESH)

    for g2 in range(ng):
        for c in range(ratio):
            unless(diagonal & (g2 == g) & (c == piece),
                   lambda g2=g2, c=c: greet(glob=jnp.int32(g2), byte=g * ratio + c))
    for s in range(nb):
        unless(diagonal & (s == b), lambda s=s: greet(glob=owner, byte=jnp.int32(s)))
    for o in range(1, nb):
        greet(byte=lax.rem(b + o, nb))
    for o in range(1, nd):
        greet(dp=lax.rem(dp + o, nd))

    row = start_ref[0, pl.ds(b, 1), :]
    i0 = lax.broadcasted_iota(jnp.int32, (slots, slots), 0)
    i1 = lax.broadcasted_iota(jnp.int32, (slots, slots), 1)
    spread = jnp.broadcast_to(row, (slots, slots))
    first = jnp.sum(jnp.where(i0 == i1, spread, 0), axis=1, keepdims=True)
    after = jnp.sum(jnp.where(i0 + 1 == i1, spread, 0), axis=1, keepdims=True)
    slot_col = lax.broadcasted_iota(jnp.int32, (slots, 1), 0)
    after = jnp.where(slot_col == slots - 1, byte_count, after)
    position = lax.broadcasted_iota(jnp.int32, (slots, byte_count), 1)
    members = jnp.where((first <= position) & (position < after), 1.0, 0.0).astype(F32)
    counts = jnp.maximum(jnp.sum(members, axis=1, keepdims=True), 1.0)
    members = members.astype(BF16)
    for c in range(ratio):
        summed = mm(members, states_ref[0, :, c * chunk:(c + 1) * chunk], 1, 0)
        pooled[c] = (summed / counts).astype(BF16)

    pl.semaphore_wait(barrier, 2 * nb - 2 * jnp.where(diagonal, 1, 0) + nb - 1 + nd - 1)

    def pool_copy(g2, c):
        return remote(pooled.at[c], pool_all.at[dp, b], s1.at[g2 * ratio + c], r1.at[b],
                      glob=jnp.int32(g2), byte=g * ratio + c)

    for g2 in range(ng):
        for c in range(ratio):
            unless(diagonal & (g2 == g) & (c == piece), lambda g2=g2, c=c: pool_copy(g2, c).start())

    @pl.when(diagonal)
    def _():
        pool_all[dp, b] = pooled[piece]

    spots = lax.broadcasted_iota(jnp.int32, (slots, total), 1)
    tiles = jnp.where(lax.rem(spots, slots) == lax.broadcasted_iota(jnp.int32, (slots, total), 0), 1.0, 0.0)
    used = jnp.where(start_ref[0] < byte_count, 1.0, 0.0)
    used = mm(used.astype(BF16), tiles.astype(BF16), 1, 0)
    lane = lax.broadcasted_iota(jnp.int32, (nb, total), 1)
    shard_of = lax.broadcasted_iota(jnp.int32, (nb, total), 0)
    mine = (lane >= shard_of * slots) & (lane < (shard_of + 1) * slots)
    used = jnp.sum(jnp.where(mine, used, 0.0), axis=0, keepdims=True)
    live = jnp.where(first < byte_count, 1.0, 0.0)
    lives = jnp.concatenate([live] * group, axis=0)
    rows = group * slots
    ids = b * slots + lax.rem(lax.broadcasted_iota(jnp.int32, (rows, total), 0), slots)
    keys = lax.broadcasted_iota(jnp.int32, (rows, total), 1)
    visible = (keys <= ids) & (jnp.broadcast_to(used, (rows, total)) > 0.5)

    for s in range(nb):
        unless(diagonal & (s == b), lambda s=s: remote(
            pooled.at[0], pool_all.at[dp, s], s1.at[0], r1.at[s], byte=b).wait_recv())

    for o in range(1, nd):
        remote(pool_all.at[dp], pool_all.at[dp], sd.at[0, o], rd.at[0, dp], dp=lax.rem(dp + o, nd)).start()

    gathered = pool_all[dp].reshape(total, chunk)
    for j in range(2):
        kv_part[:, :, j * width:(j + 1) * width] = (
            mm(gathered, w_ref[j], 1, 0).astype(BF16).reshape(nb, slots, width))

    def reduce(part, recv, whole, sa, ra, sb, rb):
        for o in range(1, nb):
            peer = lax.rem(b + o, nb)
            remote(part.at[peer], recv.at[b], sa.at[o], ra.at[b], byte=peer).start()
        acc = part[b].astype(F32)
        for o in range(1, nb):
            peer = lax.rem(b + o, nb)
            remote(part.at[peer], recv.at[peer], sa.at[o], ra.at[peer], byte=peer).wait_recv()
            acc = acc + recv[peer].astype(F32)
        whole[b] = acc.astype(BF16)
        for o in range(1, nb):
            remote(whole.at[b], whole.at[b], sb.at[o], rb.at[b], byte=lax.rem(b + o, nb)).start()
        for o in range(1, nb):
            peer = lax.rem(b + o, nb)
            remote(whole.at[b], whole.at[peer], sb.at[o], rb.at[peer], byte=peer).wait_recv()

    def sent(part, whole, recv, sa, ra, sb, rb):
        for o in range(1, nb):
            peer = lax.rem(b + o, nb)
            remote(part.at[peer], recv.at[b], sa.at[o], ra.at[b], byte=peer).wait_send()
            remote(whole.at[b], whole.at[b], sb.at[o], rb.at[b], byte=peer).wait_send()

    reduce(kv_part, kv_recv, kv_all, s2, r2, s3, r3)

    for c in range(shared):
        k = kv_all[:, :, c * HS:(c + 1) * HS].reshape(total, HS)
        v = kv_all[:, :, width + c * HS:width + (c + 1) * HS].reshape(total, HS)
        cols = [slice((c * group + h) * HS, (c * group + h + 1) * HS) for h in range(group)]
        q = jnp.concatenate([query_ref[0, :, at] for at in cols], axis=0)
        gm = jnp.concatenate([cot_ref[0, :, at] for at in cols], axis=0).astype(F32) * lives
        gm16 = gm.astype(BF16)
        scores = jnp.where(visible, mm(q, k, 1, 1) * factor, -1e30)
        top = jnp.max(scores, axis=1, keepdims=True)
        raised = jnp.where(visible, jnp.exp(scores - top), 0.0)
        prob = raised / jnp.maximum(jnp.sum(raised, axis=1, keepdims=True), 1.0)
        pb = prob.astype(BF16)
        mixed = mm(pb, v, 1, 0)
        dots = jnp.sum(gm * mixed, axis=1, keepdims=True)
        ds = (prob * (mm(gm16, v, 1, 1) - dots) * factor).astype(BF16)
        dkv_part[:, :, c * HS:(c + 1) * HS] = mm(ds, q, 0, 0).astype(BF16).reshape(nb, slots, HS)
        dkv_part[:, :, width + c * HS:width + (c + 1) * HS] = (
            mm(pb, gm16, 0, 0).astype(BF16).reshape(nb, slots, HS))
        att = (mixed * lives).astype(BF16)
        gq = mm(ds, k, 1, 0).astype(BF16)
        for h in range(group):
            att_ref[0, :, cols[h]] = att[h * slots:(h + 1) * slots]
            gq_ref[0, :, cols[h]] = gq[h * slots:(h + 1) * slots]

    reduce(dkv_part, dkv_recv, dkv_all.at[dp], s4, r4, s5, r5)
    for o in range(1, nd):
        remote(dkv_all.at[dp], dkv_all.at[dp], sd.at[1, o], rd.at[1, dp], dp=lax.rem(dp + o, nd)).start()

    dkv = dkv_all[dp].reshape(total, 2 * width)
    terms = mm(dkv[:, :width], w_ref[0], 1, 1) + mm(dkv[:, width:], w_ref[1], 1, 1)
    dpart[...] = terms.astype(BF16).reshape(nb, slots, chunk)

    def patch_copy(s):
        return remote(dpart.at[s], drecv.at[g, piece], s6.at[s], r6.at[g, piece], glob=owner, byte=jnp.int32(s))

    for s in range(nb):
        unless(diagonal & (s == b), lambda s=s: patch_copy(s).start())

    @pl.when(diagonal)
    def _():
        drecv[g, piece] = dpart[b]

    for o in range(1, nd):
        other = lax.rem(dp + o, nd)
        remote(pool_all.at[dp], pool_all.at[other], sd.at[0, o], rd.at[0, other], dp=other).wait_recv()
        remote(dkv_all.at[dp], dkv_all.at[other], sd.at[1, o], rd.at[1, other], dp=other).wait_recv()
    both = dkv_all[...].reshape(nd * total, 2 * width)
    step = math.gcd(chunk, 256)
    for at in range(0, chunk, step):
        piece_of = pool_all[:, :, :, at:at + step].reshape(nd * total, step)
        product = mm(piece_of, both, 0, 0)
        for j in range(2):
            gkv_ref[j, at:at + step, :] = product[:, j * width:(j + 1) * width]

    for g2 in range(ng):
        for c in range(ratio):
            unless(diagonal & (g2 == g) & (c == piece), lambda g2=g2, c=c: remote(
                dpart.at[0], drecv.at[g2, c], s6.at[0], r6.at[g2, c], byte=b).wait_recv())
    for c in range(ratio):
        acc = drecv[0, c].astype(F32)
        for g2 in range(1, ng):
            acc = acc + drecv[g2, c].astype(F32)
        share = (acc.astype(BF16).astype(F32) / counts).astype(BF16)
        gb_ref[0, :, c * chunk:(c + 1) * chunk] = mm(members, share, 0, 0).astype(BF16)

    for g2 in range(ng):
        for c in range(ratio):
            unless(diagonal & (g2 == g) & (c == piece), lambda g2=g2, c=c: pool_copy(g2, c).wait_send())
    sent(kv_part, kv_all, kv_recv, s2, r2, s3, r3)
    sent(dkv_part, dkv_all.at[dp], dkv_recv, s4, r4, s5, r5)
    for s in range(nb):
        unless(diagonal & (s == b), lambda s=s: patch_copy(s).wait_send())
    for o in range(1, nd):
        other = lax.rem(dp + o, nd)
        remote(pool_all.at[dp], pool_all.at[dp], sd.at[0, o], rd.at[0, dp], dp=other).wait_send()
        remote(dkv_all.at[dp], dkv_all.at[dp], sd.at[1, o], rd.at[1, dp], dp=other).wait_send()


def on_device(nd, ng, nb, byte_states, patch_start, queries, grad_out, w_kv):
    slots = patch_start.shape[2]
    chunk, width = w_kv.shape[1], w_kv.shape[2]
    ratio = nb // ng
    dma = pltpu.SemaphoreType.DMA
    vmem = pl.BlockSpec(memory_space=pltpu.VMEM)
    return pl.pallas_call(
        functools.partial(kernel, nd, ng, nb),
        out_shape=(
            jax.ShapeDtypeStruct(queries.shape, BF16),
            jax.ShapeDtypeStruct(queries.shape, BF16),
            jax.ShapeDtypeStruct(byte_states.shape, BF16),
            jax.ShapeDtypeStruct(w_kv.shape, F32),
        ),
        in_specs=[vmem] * 5,
        out_specs=(vmem,) * 4,
        scratch_shapes=[
            pltpu.VMEM((ratio, slots, chunk), BF16),
            pltpu.VMEM((nd, nb, slots, chunk), BF16),
            pltpu.VMEM((nb, slots, 2 * width), BF16),
            pltpu.VMEM((nb, slots, 2 * width), BF16),
            pltpu.VMEM((nb, slots, 2 * width), BF16),
            pltpu.VMEM((nb, slots, 2 * width), BF16),
            pltpu.VMEM((nb, slots, 2 * width), BF16),
            pltpu.VMEM((nd, nb, slots, 2 * width), BF16),
            pltpu.VMEM((nb, slots, chunk), BF16),
            pltpu.VMEM((ng, ratio, slots, chunk), BF16),
            dma((nb,)), dma((nb,)), dma((nb,)), dma((nb,)), dma((nb,)), dma((nb,)),
            dma((nb,)), dma((nb,)), dma((nb,)), dma((nb,)), dma((nb,)), dma((ng, ratio)),
            dma((2, nd)), dma((2, nd)),
        ],
        compiler_params=pltpu.CompilerParams(
            collective_id=0, has_side_effects=True, vmem_limit_bytes=48 * 1024 * 1024),
    )(byte_states, patch_start, queries, grad_out, w_kv)


def solution(mesh):
    sizes = (mesh.shape["dp"], mesh.shape["glob"], mesh.shape["byte"])
    placed = (
        P("dp", "byte", "glob"),
        P("dp", None, None),
        P("dp", "byte", "glob"),
        P("dp", "byte", "glob"),
        P(None, "byte", "glob"),
    )
    return jax.shard_map(
        functools.partial(on_device, *sizes),
        mesh=mesh,
        in_specs=placed,
        out_specs=(
            P("dp", "byte", "glob"),
            P("dp", "byte", "glob"),
            P("dp", "byte", "glob"),
            P(None, "byte", "glob"),
        ),
        check_vma=False,
    )
```

```python
import functools
import math

import jax
import jax.numpy as jnp
from jax import lax
from jax.experimental import pallas as pl
from jax.experimental.pallas import tpu as pltpu
from jax.sharding import PartitionSpec as P

HS = 128
MESH = pl.DeviceIdType.MESH
F32 = jnp.float32
BF16 = jnp.bfloat16


def mm(left, right, a, b):
    return lax.dot_general(left, right, (((a,), (b,)), ((), ())), preferred_element_type=F32)


def kernel(nd, ng, nb, states_hbm, start_hbm, query_hbm, cot_hbm, w_hbm,
           att_ref, gq_ref, gb_ref, gkv_ref,
           states_ref, start_ref, query_ref, cot_ref, w_ref, loads,
           pooled, quarter, pool_all, kv_part, kv_recv, kv_all, dkv_part, dkv_recv, dkv_all, dpart, dterm, dsum, drecv,
           s0, r0, s7, r7, s1, r1, s2, r2, s3, r3, s4, r4, s5, r5, s6, r6, sd, rd):
    fetch = [pltpu.make_async_copy(src, dst, loads.at[at]) for at, (src, dst) in enumerate((
        (start_hbm, start_ref), (states_hbm, states_ref), (w_hbm, w_ref),
        (query_hbm, query_ref), (cot_hbm, cot_ref)))]
    for load in fetch:
        load.start()
    dp = lax.axis_index("dp")
    g = lax.axis_index("glob")
    b = lax.axis_index("byte")
    ratio = nb // ng
    owner = b // ratio
    piece = lax.rem(b, ratio)
    diagonal = g == owner
    byte_count = states_ref.shape[1]
    slots = start_ref.shape[2]
    total = nb * slots
    chunk = w_ref.shape[1]
    width = w_ref.shape[2]
    shared = width // HS
    part = chunk // ng
    group = query_ref.shape[2] // width
    factor = 1.0 / math.sqrt(HS)

    def remote(src, dst, send, recv, **where):
        return pltpu.make_async_remote_copy(
            src_ref=src, dst_ref=dst, send_sem=send, recv_sem=recv,
            device_id=where, device_id_type=MESH)

    def unless(cond, fn):
        pl.when(jnp.logical_not(cond))(fn)

    barrier = pltpu.get_barrier_semaphore()

    def greet(**where):
        pl.semaphore_signal(barrier, inc=1, device_id=where, device_id_type=MESH)

    for g2 in range(ng):
        for c in range(ratio):
            unless(diagonal & (g2 == g) & (c == piece),
                   lambda g2=g2, c=c: greet(glob=jnp.int32(g2), byte=g * ratio + c))
    for s in range(nb):
        unless(diagonal & (s == b), lambda s=s: greet(glob=owner, byte=jnp.int32(s)))
    for o in range(1, nb):
        greet(byte=lax.rem(b + o, nb))
    for o in range(1, ng):
        greet(glob=lax.rem(g + o, ng))
    for o in range(1, nd):
        greet(dp=lax.rem(dp + o, nd))
    fetch[0].wait()
    fetch[1].wait()

    row = start_ref[0, pl.ds(b, 1), :]
    i0 = lax.broadcasted_iota(jnp.int32, (slots, slots), 0)
    i1 = lax.broadcasted_iota(jnp.int32, (slots, slots), 1)
    spread = jnp.broadcast_to(row, (slots, slots))
    first = jnp.sum(jnp.where(i0 == i1, spread, 0), axis=1, keepdims=True)
    after = jnp.sum(jnp.where(i0 + 1 == i1, spread, 0), axis=1, keepdims=True)
    slot_col = lax.broadcasted_iota(jnp.int32, (slots, 1), 0)
    after = jnp.where(slot_col == slots - 1, byte_count, after)
    position = lax.broadcasted_iota(jnp.int32, (slots, byte_count), 1)
    members = jnp.where((first <= position) & (position < after), 1.0, 0.0).astype(F32)
    counts = jnp.maximum(jnp.sum(members, axis=1, keepdims=True), 1.0)
    members = members.astype(BF16)
    for c in range(ratio):
        summed = mm(members, states_ref[0, :, c * chunk:(c + 1) * chunk], 1, 0)
        means = (summed / counts).astype(BF16)
        for i in range(ng):
            pooled[c, i] = means[:, i * part:(i + 1) * part]

    pl.semaphore_wait(barrier, 2 * nb - 2 * jnp.where(diagonal, 1, 0) + nb - 1 + ng - 1 + nd - 1)

    def pool_copy(g2, c):
        return remote(pooled.at[c, g2], quarter.at[b], s1.at[g2 * ratio + c], r1.at[b],
                      glob=jnp.int32(g2), byte=g * ratio + c)

    for g2 in range(ng):
        for c in range(ratio):
            unless(diagonal & (g2 == g) & (c == piece), lambda g2=g2, c=c: pool_copy(g2, c).start())

    @pl.when(diagonal)
    def _():
        quarter[b] = pooled[piece, g]

    spots = lax.broadcasted_iota(jnp.int32, (slots, total), 1)
    tiles = jnp.where(lax.rem(spots, slots) == lax.broadcasted_iota(jnp.int32, (slots, total), 0), 1.0, 0.0)
    used = jnp.where(start_ref[0] < byte_count, 1.0, 0.0)
    used = mm(used.astype(BF16), tiles.astype(BF16), 1, 0)
    lane = lax.broadcasted_iota(jnp.int32, (nb, total), 1)
    shard_of = lax.broadcasted_iota(jnp.int32, (nb, total), 0)
    mine = (lane >= shard_of * slots) & (lane < (shard_of + 1) * slots)
    used = jnp.sum(jnp.where(mine, used, 0.0), axis=0, keepdims=True)
    live = jnp.where(first < byte_count, 1.0, 0.0)
    lives = jnp.concatenate([live] * group, axis=0)
    rows = group * slots
    ids = b * slots + lax.rem(lax.broadcasted_iota(jnp.int32, (rows, total), 0), slots)
    keys = lax.broadcasted_iota(jnp.int32, (rows, total), 1)
    visible = (keys <= ids) & (jnp.broadcast_to(used, (rows, total)) > 0.5)

    for s in range(nb):
        unless(diagonal & (s == b), lambda s=s: remote(
            pooled.at[0, 0], quarter.at[s], s1.at[0], r1.at[s], byte=b).wait_recv())

    def plane_copy(o, slot):
        return remote(quarter, pool_all.at[dp, slot], s0.at[o], r0.at[slot], glob=lax.rem(g + o, ng))

    for o in range(1, ng):
        plane_copy(o, g).start()
    pool_all[dp, g] = quarter[...]
    fetch[2].wait()
    for o in range(1, ng):
        plane_copy(o, lax.rem(g + o, ng)).wait_recv()

    for o in range(1, nd):
        remote(pool_all.at[dp], pool_all.at[dp], sd.at[0, o], rd.at[0, dp], dp=lax.rem(dp + o, nd)).start()

    for j in range(2):
        acc = mm(pool_all[dp, 0].reshape(total, part), w_ref[j, :part], 1, 0)
        for i in range(1, ng):
            acc = acc + mm(pool_all[dp, i].reshape(total, part), w_ref[j, i * part:(i + 1) * part], 1, 0)
        kv_part[:, :, j * width:(j + 1) * width] = acc.astype(BF16).reshape(nb, slots, width)
    fetch[3].wait()
    fetch[4].wait()

    def reduce(part, recv, whole, sa, ra, sb, rb):
        for o in range(1, nb):
            peer = lax.rem(b + o, nb)
            remote(part.at[peer], recv.at[b], sa.at[o], ra.at[b], byte=peer).start()
        acc = part[b].astype(F32)
        for o in range(1, nb):
            peer = lax.rem(b + o, nb)
            remote(part.at[peer], recv.at[peer], sa.at[o], ra.at[peer], byte=peer).wait_recv()
            acc = acc + recv[peer].astype(F32)
        whole[b] = acc.astype(BF16)
        for o in range(1, nb):
            remote(whole.at[b], whole.at[b], sb.at[o], rb.at[b], byte=lax.rem(b + o, nb)).start()
        for o in range(1, nb):
            peer = lax.rem(b + o, nb)
            remote(whole.at[b], whole.at[peer], sb.at[o], rb.at[peer], byte=peer).wait_recv()

    def sent(part, whole, recv, sa, ra, sb, rb):
        for o in range(1, nb):
            peer = lax.rem(b + o, nb)
            remote(part.at[peer], recv.at[b], sa.at[o], ra.at[b], byte=peer).wait_send()
            remote(whole.at[b], whole.at[b], sb.at[o], rb.at[b], byte=peer).wait_send()

    reduce(kv_part, kv_recv, kv_all, s2, r2, s3, r3)

    for c in range(shared):
        k = kv_all[:, :, c * HS:(c + 1) * HS].reshape(total, HS)
        v = kv_all[:, :, width + c * HS:width + (c + 1) * HS].reshape(total, HS)
        cols = [slice((c * group + h) * HS, (c * group + h + 1) * HS) for h in range(group)]
        q = jnp.concatenate([query_ref[0, :, at] for at in cols], axis=0)
        gm = jnp.concatenate([cot_ref[0, :, at] for at in cols], axis=0).astype(F32) * lives
        gm16 = gm.astype(BF16)
        scores = jnp.where(visible, mm(q, k, 1, 1) * factor, -1e30)
        top = jnp.max(scores, axis=1, keepdims=True)
        raised = jnp.where(visible, jnp.exp(scores - top), 0.0)
        prob = raised / jnp.maximum(jnp.sum(raised, axis=1, keepdims=True), 1.0)
        pb = prob.astype(BF16)
        mixed = mm(pb, v, 1, 0)
        dots = jnp.sum(gm * mixed, axis=1, keepdims=True)
        ds = (prob * (mm(gm16, v, 1, 1) - dots) * factor).astype(BF16)
        dkv_part[:, :, c * HS:(c + 1) * HS] = mm(ds, q, 0, 0).astype(BF16).reshape(nb, slots, HS)
        dkv_part[:, :, width + c * HS:width + (c + 1) * HS] = (
            mm(pb, gm16, 0, 0).astype(BF16).reshape(nb, slots, HS))
        att = (mixed * lives).astype(BF16)
        gq = mm(ds, k, 1, 0).astype(BF16)
        for h in range(group):
            att_ref[0, :, cols[h]] = att[h * slots:(h + 1) * slots]
            gq_ref[0, :, cols[h]] = gq[h * slots:(h + 1) * slots]

    reduce(dkv_part, dkv_recv, dkv_all.at[dp], s4, r4, s5, r5)
    for o in range(1, nd):
        remote(dkv_all.at[dp], dkv_all.at[dp], sd.at[1, o], rd.at[1, dp], dp=lax.rem(dp + o, nd)).start()

    dkv = dkv_all[dp].reshape(total, 2 * width)
    terms = mm(dkv[:, :width], w_ref[0], 1, 1) + mm(dkv[:, width:], w_ref[1], 1, 1)
    for i in range(ng):
        dpart[i] = terms[:, i * part:(i + 1) * part].astype(BF16).reshape(nb, slots, part)

    def cut_copy(o, slot):
        peer = lax.rem(g + o, ng)
        return remote(dpart.at[peer], dterm.at[slot], s7.at[o], r7.at[slot], glob=peer)

    for o in range(1, ng):
        cut_copy(o, g).start()

    for o in range(1, nd):
        other = lax.rem(dp + o, nd)
        remote(pool_all.at[dp], pool_all.at[other], sd.at[0, o], rd.at[0, other], dp=other).wait_recv()
        remote(dkv_all.at[dp], dkv_all.at[other], sd.at[1, o], rd.at[1, other], dp=other).wait_recv()
    both = dkv_all[...].reshape(nd * total, 2 * width)
    for i in range(ng):
        product = mm(pool_all[:, i].reshape(nd * total, part), both, 0, 0)
        for j in range(2):
            gkv_ref[j, i * part:(i + 1) * part, :] = product[:, j * width:(j + 1) * width]

    acc = dpart[g].astype(F32)
    for o in range(1, ng):
        peer = lax.rem(g + o, ng)
        cut_copy(o, peer).wait_recv()
        acc = acc + dterm[peer].astype(F32)
    dsum[...] = acc.astype(BF16)

    def patch_copy(s):
        return remote(dsum.at[s], drecv.at[g, piece], s6.at[s], r6.at[g, piece], glob=owner, byte=jnp.int32(s))

    for s in range(nb):
        unless(diagonal & (s == b), lambda s=s: patch_copy(s).start())

    @pl.when(diagonal)
    def _():
        drecv[g, piece] = dsum[b]

    for g2 in range(ng):
        for c in range(ratio):
            unless(diagonal & (g2 == g) & (c == piece), lambda g2=g2, c=c: remote(
                dsum.at[0], drecv.at[g2, c], s6.at[0], r6.at[g2, c], byte=b).wait_recv())
    for c in range(ratio):
        for i in range(ng):
            share = (drecv[i, c].astype(F32) / counts).astype(BF16)
            first_col = c * chunk + i * part
            gb_ref[0, :, first_col:first_col + part] = mm(members, share, 0, 0).astype(BF16)

    for g2 in range(ng):
        for c in range(ratio):
            unless(diagonal & (g2 == g) & (c == piece), lambda g2=g2, c=c: pool_copy(g2, c).wait_send())
    sent(kv_part, kv_all, kv_recv, s2, r2, s3, r3)
    sent(dkv_part, dkv_all.at[dp], dkv_recv, s4, r4, s5, r5)
    for o in range(1, ng):
        plane_copy(o, g).wait_send()
        cut_copy(o, g).wait_send()
    for s in range(nb):
        unless(diagonal & (s == b), lambda s=s: patch_copy(s).wait_send())
    for o in range(1, nd):
        other = lax.rem(dp + o, nd)
        remote(pool_all.at[dp], pool_all.at[dp], sd.at[0, o], rd.at[0, dp], dp=other).wait_send()
        remote(dkv_all.at[dp], dkv_all.at[dp], sd.at[1, o], rd.at[1, dp], dp=other).wait_send()


def on_device(nd, ng, nb, byte_states, patch_start, queries, grad_out, w_kv):
    slots = patch_start.shape[2]
    chunk, width = w_kv.shape[1], w_kv.shape[2]
    ratio = nb // ng
    part = chunk // ng
    dma = pltpu.SemaphoreType.DMA
    vmem = pl.BlockSpec(memory_space=pltpu.VMEM)
    return pl.pallas_call(
        functools.partial(kernel, nd, ng, nb),
        out_shape=(
            jax.ShapeDtypeStruct(queries.shape, BF16),
            jax.ShapeDtypeStruct(queries.shape, BF16),
            jax.ShapeDtypeStruct(byte_states.shape, BF16),
            jax.ShapeDtypeStruct(w_kv.shape, F32),
        ),
        in_specs=[pl.BlockSpec(memory_space=pltpu.HBM)] * 5,
        out_specs=(vmem,) * 4,
        scratch_shapes=[
            pltpu.VMEM(byte_states.shape, BF16),
            pltpu.VMEM(patch_start.shape, patch_start.dtype),
            pltpu.VMEM(queries.shape, BF16),
            pltpu.VMEM(grad_out.shape, BF16),
            pltpu.VMEM(w_kv.shape, BF16),
            dma((5,)),
            pltpu.VMEM((ratio, ng, slots, part), BF16),
            pltpu.VMEM((nb, slots, part), BF16),
            pltpu.VMEM((nd, ng, nb, slots, part), BF16),
            pltpu.VMEM((nb, slots, 2 * width), BF16),
            pltpu.VMEM((nb, slots, 2 * width), BF16),
            pltpu.VMEM((nb, slots, 2 * width), BF16),
            pltpu.VMEM((nb, slots, 2 * width), BF16),
            pltpu.VMEM((nb, slots, 2 * width), BF16),
            pltpu.VMEM((nd, nb, slots, 2 * width), BF16),
            pltpu.VMEM((ng, nb, slots, part), BF16),
            pltpu.VMEM((ng, nb, slots, part), BF16),
            pltpu.VMEM((nb, slots, part), BF16),
            pltpu.VMEM((ng, ratio, slots, part), BF16),
            dma((ng,)), dma((ng,)), dma((ng,)), dma((ng,)),
            dma((nb,)), dma((nb,)), dma((nb,)), dma((nb,)), dma((nb,)), dma((nb,)),
            dma((nb,)), dma((nb,)), dma((nb,)), dma((nb,)), dma((nb,)), dma((ng, ratio)),
            dma((2, nd)), dma((2, nd)),
        ],
        compiler_params=pltpu.CompilerParams(
            collective_id=0, has_side_effects=True, vmem_limit_bytes=48 * 1024 * 1024),
    )(byte_states, patch_start, queries, grad_out, w_kv)


def solution(mesh):
    sizes = (mesh.shape["dp"], mesh.shape["glob"], mesh.shape["byte"])
    placed = (
        P("dp", "byte", "glob"),
        P("dp", None, None),
        P("dp", "byte", "glob"),
        P("dp", "byte", "glob"),
        P(None, "byte", "glob"),
    )
    return jax.shard_map(
        functools.partial(on_device, *sizes),
        mesh=mesh,
        in_specs=placed,
        out_specs=(
            P("dp", "byte", "glob"),
            P("dp", "byte", "glob"),
            P("dp", "byte", "glob"),
            P(None, "byte", "glob"),
        ),
        check_vma=False,
    )
```

```python
import functools
import math

import jax
import jax.numpy as jnp
from jax import lax
from jax.experimental import pallas as pl
from jax.experimental.pallas import tpu as pltpu
from jax.sharding import PartitionSpec as P

HS = 128
MESH = pl.DeviceIdType.MESH
F32 = jnp.float32
BF16 = jnp.bfloat16


def mm(left, right, a, b):
    return lax.dot_general(left, right, (((a,), (b,)), ((), ())), preferred_element_type=F32)


def kernel(nd, ng, nb, states_hbm, start_hbm, query_hbm, cot_hbm, w_hbm,
           att_hbm, gq_hbm, gb_hbm, gkv_hbm,
           states_ref, start_ref, query_ref, cot_ref, w_ref, wt_ref, loads,
           att_ref, gq_ref, gb_ref, gkv_ref, stores,
           pooled, quarter, pool_all, kv_part, kv_recv, kv_all, dkv_part, dkv_recv, dkv_all, dpart, dterm, dsum, drecv,
           s0, r0, s7, r7, s1, r1, s2, r2, s3, r3, s4, r4, s5, r5, s6, r6, sd, rd):
    fetch = [pltpu.make_async_copy(src, dst, loads.at[at]) for at, (src, dst) in enumerate((
        (start_hbm, start_ref), (states_hbm, states_ref),
        (w_hbm.at[0], w_ref.at[:, :w_hbm.shape[2]]), (w_hbm.at[1], w_ref.at[:, w_hbm.shape[2]:]),
        (query_hbm, query_ref), (cot_hbm, cot_ref)))]
    give = [pltpu.make_async_copy(src, dst, stores.at[at]) for at, (src, dst) in enumerate((
        (att_ref, att_hbm), (gq_ref, gq_hbm), (gb_ref, gb_hbm), (gkv_ref, gkv_hbm)))]
    for load in fetch:
        load.start()
    dp = lax.axis_index("dp")
    g = lax.axis_index("glob")
    b = lax.axis_index("byte")
    ratio = nb // ng
    owner = b // ratio
    piece = lax.rem(b, ratio)
    diagonal = g == owner
    byte_count = states_ref.shape[1]
    slots = start_ref.shape[2]
    total = nb * slots
    chunk = w_ref.shape[0]
    width = w_ref.shape[1] // 2
    shared = width // HS
    part = chunk // ng
    group = query_ref.shape[2] // width
    factor = 1.0 / math.sqrt(HS)

    def remote(src, dst, send, recv, **where):
        return pltpu.make_async_remote_copy(
            src_ref=src, dst_ref=dst, send_sem=send, recv_sem=recv,
            device_id=where, device_id_type=MESH)

    def unless(cond, fn):
        pl.when(jnp.logical_not(cond))(fn)

    barrier = pltpu.get_barrier_semaphore()

    def greet(**where):
        pl.semaphore_signal(barrier, inc=1, device_id=where, device_id_type=MESH)

    for g2 in range(ng):
        for c in range(ratio):
            unless(diagonal & (g2 == g) & (c == piece),
                   lambda g2=g2, c=c: greet(glob=jnp.int32(g2), byte=g * ratio + c))
    for s in range(nb):
        unless(diagonal & (s == b), lambda s=s: greet(glob=owner, byte=jnp.int32(s)))
    for o in range(1, nb):
        greet(byte=lax.rem(b + o, nb))
    for o in range(1, ng):
        greet(glob=lax.rem(g + o, ng))
    for o in range(1, nd):
        greet(dp=lax.rem(dp + o, nd))
    fetch[0].wait()
    fetch[1].wait()

    row = start_ref[0, pl.ds(b, 1), :]
    i0 = lax.broadcasted_iota(jnp.int32, (slots, slots), 0)
    i1 = lax.broadcasted_iota(jnp.int32, (slots, slots), 1)
    spread = jnp.broadcast_to(row, (slots, slots))
    first = jnp.sum(jnp.where(i0 == i1, spread, 0), axis=1, keepdims=True)
    after = jnp.sum(jnp.where(i0 + 1 == i1, spread, 0), axis=1, keepdims=True)
    slot_col = lax.broadcasted_iota(jnp.int32, (slots, 1), 0)
    after = jnp.where(slot_col == slots - 1, byte_count, after)
    position = lax.broadcasted_iota(jnp.int32, (slots, byte_count), 1)
    members = jnp.where((first <= position) & (position < after), 1.0, 0.0).astype(F32)
    counts = jnp.maximum(jnp.sum(members, axis=1, keepdims=True), 1.0)
    members = members.astype(BF16)
    for c in range(ratio):
        summed = mm(members, states_ref[0, :, c * chunk:(c + 1) * chunk], 1, 0)
        means = (summed / counts).astype(BF16)
        for i in range(ng):
            pooled[c, i] = means[:, i * part:(i + 1) * part]

    pl.semaphore_wait(barrier, 2 * nb - 2 * jnp.where(diagonal, 1, 0) + nb - 1 + ng - 1 + nd - 1)

    def pool_copy(g2, c):
        return remote(pooled.at[c, g2], quarter.at[b], s1.at[g2 * ratio + c], r1.at[b],
                      glob=jnp.int32(g2), byte=g * ratio + c)

    for g2 in range(ng):
        for c in range(ratio):
            unless(diagonal & (g2 == g) & (c == piece), lambda g2=g2, c=c: pool_copy(g2, c).start())

    @pl.when(diagonal)
    def _():
        quarter[b] = pooled[piece, g]

    spots = lax.broadcasted_iota(jnp.int32, (slots, total), 1)
    tiles = jnp.where(lax.rem(spots, slots) == lax.broadcasted_iota(jnp.int32, (slots, total), 0), 1.0, 0.0)
    used = jnp.where(start_ref[0] < byte_count, 1.0, 0.0)
    used = mm(used.astype(BF16), tiles.astype(BF16), 1, 0)
    lane = lax.broadcasted_iota(jnp.int32, (nb, total), 1)
    shard_of = lax.broadcasted_iota(jnp.int32, (nb, total), 0)
    mine = (lane >= shard_of * slots) & (lane < (shard_of + 1) * slots)
    used = jnp.sum(jnp.where(mine, used, 0.0), axis=0, keepdims=True)
    live = jnp.where(first < byte_count, 1.0, 0.0)
    lives = jnp.concatenate([live] * group, axis=0)
    rows = group * slots
    ids = b * slots + lax.rem(lax.broadcasted_iota(jnp.int32, (rows, total), 0), slots)
    keys = lax.broadcasted_iota(jnp.int32, (rows, total), 1)
    visible = (keys <= ids) & (jnp.broadcast_to(used, (rows, total)) > 0.5)

    heads = []
    fetch[4].wait()
    fetch[5].wait()
    for c in range(shared):
        cols = [slice((c * group + h) * HS, (c * group + h + 1) * HS) for h in range(group)]
        q = jnp.concatenate([query_ref[0, :, at] for at in cols], axis=0)
        gm = jnp.concatenate([cot_ref[0, :, at] for at in cols], axis=0).astype(F32) * lives
        heads.append((cols, q, gm, gm.astype(BF16)))
    fetch[2].wait()
    fetch[3].wait()
    wt_ref[...] = w_ref[...].T

    for s in range(nb):
        unless(diagonal & (s == b), lambda s=s: remote(
            pooled.at[0, 0], quarter.at[s], s1.at[0], r1.at[s], byte=b).wait_recv())

    def plane_copy(o, slot):
        return remote(quarter, pool_all.at[dp, slot], s0.at[o], r0.at[slot], glob=lax.rem(g + o, ng))

    for o in range(1, ng):
        plane_copy(o, g).start()
    pool_all[dp, g] = quarter[...]
    for o in range(1, ng):
        plane_copy(o, lax.rem(g + o, ng)).wait_recv()

    for o in range(1, nd):
        remote(pool_all.at[dp], pool_all.at[dp], sd.at[0, o], rd.at[0, dp], dp=lax.rem(dp + o, nd)).start()

    acc = mm(pool_all[dp, 0].reshape(total, part), w_ref[:part], 1, 0)
    for i in range(1, ng):
        acc = acc + mm(pool_all[dp, i].reshape(total, part), w_ref[i * part:(i + 1) * part], 1, 0)
    kv_part[...] = acc.astype(BF16).reshape(nb, slots, 2 * width)

    def reduce(part, recv, whole, sa, ra, sb, rb, beside=None):
        for o in range(1, nb):
            peer = lax.rem(b + o, nb)
            remote(part.at[peer], recv.at[b], sa.at[o], ra.at[b], byte=peer).start()
        if beside is not None:
            beside()
        acc = part[b].astype(F32)
        for o in range(1, nb):
            peer = lax.rem(b + o, nb)
            remote(part.at[peer], recv.at[peer], sa.at[o], ra.at[peer], byte=peer).wait_recv()
            acc = acc + recv[peer].astype(F32)
        whole[b] = acc.astype(BF16)
        for o in range(1, nb):
            remote(whole.at[b], whole.at[b], sb.at[o], rb.at[b], byte=lax.rem(b + o, nb)).start()
        for o in range(1, nb):
            peer = lax.rem(b + o, nb)
            remote(whole.at[b], whole.at[peer], sb.at[o], rb.at[peer], byte=peer).wait_recv()

    def sent(part, whole, recv, sa, ra, sb, rb):
        for o in range(1, nb):
            peer = lax.rem(b + o, nb)
            remote(part.at[peer], recv.at[b], sa.at[o], ra.at[b], byte=peer).wait_send()
            remote(whole.at[b], whole.at[b], sb.at[o], rb.at[b], byte=peer).wait_send()

    reduce(kv_part, kv_recv, kv_all, s2, r2, s3, r3)

    done = []
    for c in range(shared):
        k = kv_all[:, :, c * HS:(c + 1) * HS].reshape(total, HS)
        v = kv_all[:, :, width + c * HS:width + (c + 1) * HS].reshape(total, HS)
        cols, q, gm, gm16 = heads[c]
        scores = jnp.where(visible, mm(q, k, 1, 1) * factor, -1e30)
        top = jnp.max(scores, axis=1, keepdims=True)
        raised = jnp.where(visible, jnp.exp(scores - top), 0.0)
        prob = raised / jnp.maximum(jnp.sum(raised, axis=1, keepdims=True), 1.0)
        pb = prob.astype(BF16)
        mixed = mm(pb, v, 1, 0)
        dots = jnp.sum(gm * mixed, axis=1, keepdims=True)
        ds = (prob * (mm(gm16, v, 1, 1) - dots) * factor).astype(BF16)
        dkv_part[:, :, c * HS:(c + 1) * HS] = mm(ds, q, 0, 0).astype(BF16).reshape(nb, slots, HS)
        dkv_part[:, :, width + c * HS:width + (c + 1) * HS] = (
            mm(pb, gm16, 0, 0).astype(BF16).reshape(nb, slots, HS))
        done.append((cols, mixed, ds, k))

    def outputs():
        for cols, mixed, ds, k in done:
            att = (mixed * lives).astype(BF16)
            gq = mm(ds, k, 1, 0).astype(BF16)
            for h in range(group):
                att_ref[0, :, cols[h]] = att[h * slots:(h + 1) * slots]
                gq_ref[0, :, cols[h]] = gq[h * slots:(h + 1) * slots]
        give[0].start()
        give[1].start()

    reduce(dkv_part, dkv_recv, dkv_all.at[dp], s4, r4, s5, r5, outputs)
    for o in range(1, nd):
        remote(dkv_all.at[dp], dkv_all.at[dp], sd.at[1, o], rd.at[1, dp], dp=lax.rem(dp + o, nd)).start()

    dkv = dkv_all[dp].reshape(total, 2 * width)
    terms = mm(dkv, wt_ref[...], 1, 0)
    for i in range(ng):
        dpart[i] = terms[:, i * part:(i + 1) * part].astype(BF16).reshape(nb, slots, part)

    def cut_copy(o, slot):
        peer = lax.rem(g + o, ng)
        return remote(dpart.at[peer], dterm.at[slot], s7.at[o], r7.at[slot], glob=peer)

    for o in range(1, ng):
        cut_copy(o, g).start()

    for o in range(1, nd):
        other = lax.rem(dp + o, nd)
        remote(pool_all.at[dp], pool_all.at[other], sd.at[0, o], rd.at[0, other], dp=other).wait_recv()
        remote(dkv_all.at[dp], dkv_all.at[other], sd.at[1, o], rd.at[1, other], dp=other).wait_recv()
    both = dkv_all[...].reshape(nd * total, 2 * width)
    def weights(i):
        product = mm(pool_all[:, i].reshape(nd * total, part), both, 0, 0)
        for j in range(2):
            gkv_ref[j, i * part:(i + 1) * part, :] = product[:, j * width:(j + 1) * width]

    for i in range(ng // 2):
        weights(i)

    acc = dpart[g].astype(F32)
    for o in range(1, ng):
        peer = lax.rem(g + o, ng)
        cut_copy(o, peer).wait_recv()
        acc = acc + dterm[peer].astype(F32)
    dsum[...] = acc.astype(BF16)

    def patch_copy(s):
        return remote(dsum.at[s], drecv.at[g, piece], s6.at[s], r6.at[g, piece], glob=owner, byte=jnp.int32(s))

    for s in range(nb):
        unless(diagonal & (s == b), lambda s=s: patch_copy(s).start())

    @pl.when(diagonal)
    def _():
        drecv[g, piece] = dsum[b]

    for i in range(ng // 2, ng):
        weights(i)
    give[3].start()

    for g2 in range(ng):
        for c in range(ratio):
            unless(diagonal & (g2 == g) & (c == piece), lambda g2=g2, c=c: remote(
                dsum.at[0], drecv.at[g2, c], s6.at[0], r6.at[g2, c], byte=b).wait_recv())
    for c in range(ratio):
        for i in range(ng):
            share = (drecv[i, c].astype(F32) / counts).astype(BF16)
            first_col = c * chunk + i * part
            gb_ref[0, :, first_col:first_col + part] = mm(members, share, 0, 0).astype(BF16)
    give[2].start()

    for g2 in range(ng):
        for c in range(ratio):
            unless(diagonal & (g2 == g) & (c == piece), lambda g2=g2, c=c: pool_copy(g2, c).wait_send())
    sent(kv_part, kv_all, kv_recv, s2, r2, s3, r3)
    sent(dkv_part, dkv_all.at[dp], dkv_recv, s4, r4, s5, r5)
    for o in range(1, ng):
        plane_copy(o, g).wait_send()
        cut_copy(o, g).wait_send()
    for s in range(nb):
        unless(diagonal & (s == b), lambda s=s: patch_copy(s).wait_send())
    for o in range(1, nd):
        other = lax.rem(dp + o, nd)
        remote(pool_all.at[dp], pool_all.at[dp], sd.at[0, o], rd.at[0, dp], dp=other).wait_send()
        remote(dkv_all.at[dp], dkv_all.at[dp], sd.at[1, o], rd.at[1, dp], dp=other).wait_send()
    for store in give:
        store.wait()


def hand_on(*refs):
    count = len(refs) // 2
    sems = refs[-1]
    moves = [pltpu.make_async_copy(refs[at], refs[count + at], sems.at[at]) for at in range(count)]
    for move in moves:
        move.start()
    for move in moves:
        move.wait()


def on_device(nd, ng, nb, byte_states, patch_start, queries, grad_out, w_kv):
    slots = patch_start.shape[2]
    chunk, width = w_kv.shape[1], w_kv.shape[2]
    ratio = nb // ng
    part = chunk // ng
    dma = pltpu.SemaphoreType.DMA
    hbm = pl.BlockSpec(memory_space=pltpu.HBM)
    found = pl.pallas_call(
        functools.partial(kernel, nd, ng, nb),
        out_shape=(
            jax.ShapeDtypeStruct(queries.shape, BF16),
            jax.ShapeDtypeStruct(queries.shape, BF16),
            jax.ShapeDtypeStruct(byte_states.shape, BF16),
            jax.ShapeDtypeStruct(w_kv.shape, F32),
        ),
        in_specs=[hbm] * 5,
        out_specs=(hbm,) * 4,
        scratch_shapes=[
            pltpu.VMEM(byte_states.shape, BF16),
            pltpu.VMEM(patch_start.shape, patch_start.dtype),
            pltpu.VMEM(queries.shape, BF16),
            pltpu.VMEM(grad_out.shape, BF16),
            pltpu.VMEM((chunk, 2 * width), BF16),
            pltpu.VMEM((2 * width, chunk), BF16),
            dma((6,)),
            pltpu.VMEM(queries.shape, BF16),
            pltpu.VMEM(queries.shape, BF16),
            pltpu.VMEM(byte_states.shape, BF16),
            pltpu.VMEM(w_kv.shape, F32),
            dma((4,)),
            pltpu.VMEM((ratio, ng, slots, part), BF16),
            pltpu.VMEM((nb, slots, part), BF16),
            pltpu.VMEM((nd, ng, nb, slots, part), BF16),
            pltpu.VMEM((nb, slots, 2 * width), BF16),
            pltpu.VMEM((nb, slots, 2 * width), BF16),
            pltpu.VMEM((nb, slots, 2 * width), BF16),
            pltpu.VMEM((nb, slots, 2 * width), BF16),
            pltpu.VMEM((nb, slots, 2 * width), BF16),
            pltpu.VMEM((nd, nb, slots, 2 * width), BF16),
            pltpu.VMEM((ng, nb, slots, part), BF16),
            pltpu.VMEM((ng, nb, slots, part), BF16),
            pltpu.VMEM((nb, slots, part), BF16),
            pltpu.VMEM((ng, ratio, slots, part), BF16),
            dma((ng,)), dma((ng,)), dma((ng,)), dma((ng,)),
            dma((nb,)), dma((nb,)), dma((nb,)), dma((nb,)), dma((nb,)), dma((nb,)),
            dma((nb,)), dma((nb,)), dma((nb,)), dma((nb,)), dma((nb,)), dma((ng, ratio)),
            dma((2, nd)), dma((2, nd)),
        ],
        compiler_params=pltpu.CompilerParams(
            collective_id=0, has_side_effects=True, vmem_limit_bytes=56 * 1024 * 1024),
    )(byte_states, patch_start, queries, grad_out, w_kv)
    return pl.pallas_call(
        hand_on,
        out_shape=tuple(jax.ShapeDtypeStruct(one.shape, one.dtype) for one in found),
        in_specs=[pl.BlockSpec(memory_space=pl.ANY)] * 4,
        out_specs=(hbm,) * 4,
        scratch_shapes=[dma((4,))],
    )(*found)


def solution(mesh):
    sizes = (mesh.shape["dp"], mesh.shape["glob"], mesh.shape["byte"])
    placed = (
        P("dp", "byte", "glob"),
        P("dp", None, None),
        P("dp", "byte", "glob"),
        P("dp", "byte", "glob"),
        P(None, "byte", "glob"),
    )
    return jax.shard_map(
        functools.partial(on_device, *sizes),
        mesh=mesh,
        in_specs=placed,
        out_specs=(
            P("dp", "byte", "glob"),
            P("dp", "byte", "glob"),
            P("dp", "byte", "glob"),
            P(None, "byte", "glob"),
        ),
        check_vma=False,
    )
```

```python
import functools
import math

import jax
import jax.numpy as jnp
from jax import lax
from jax.experimental import pallas as pl
from jax.experimental.pallas import tpu as pltpu
from jax.sharding import PartitionSpec as P

HS = 128
MESH = pl.DeviceIdType.MESH
F32 = jnp.float32
BF16 = jnp.bfloat16


def mm(left, right, a, b):
    return lax.dot_general(left, right, (((a,), (b,)), ((), ())), preferred_element_type=F32)


def kernel(nd, ng, nb, states_hbm, start_hbm, query_hbm, cot_hbm, w_hbm,
           att_hbm, gq_hbm, gb_hbm, gkv_hbm,
           states_ref, start_ref, query_ref, cot_ref, w_ref, wt_ref, loads,
           att_ref, gq_ref, gb_ref, gkv_ref, stores,
           pooled, quarter, pool_all, kv_part, kv_recv, kv_all, dkv_part, dkv_recv, dkv_all, dpart, dterm, dsum, drecv,
           s0, r0, s7, r7, s1, r1, s2, r2, s3, r3, s4, r4, s5, r5, s6, r6, sd, rd):
    fetch = [pltpu.make_async_copy(src, dst, loads.at[at]) for at, (src, dst) in enumerate((
        (start_hbm, start_ref), (states_hbm, states_ref),
        (w_hbm.at[0], w_ref.at[:, :w_hbm.shape[2]]), (w_hbm.at[1], w_ref.at[:, w_hbm.shape[2]:]),
        (query_hbm, query_ref), (cot_hbm, cot_ref)))]
    give = [pltpu.make_async_copy(src, dst, stores.at[at]) for at, (src, dst) in enumerate((
        (att_ref, att_hbm), (gq_ref, gq_hbm), (gb_ref, gb_hbm), (gkv_ref, gkv_hbm)))]
    for load in fetch:
        load.start()
    dp = lax.axis_index("dp")
    g = lax.axis_index("glob")
    b = lax.axis_index("byte")
    ratio = nb // ng
    owner = b // ratio
    piece = lax.rem(b, ratio)
    diagonal = g == owner
    byte_count = states_ref.shape[1]
    slots = start_ref.shape[2]
    total = nb * slots
    chunk = w_ref.shape[0]
    width = w_ref.shape[1] // 2
    shared = width // HS
    part = chunk // ng
    group = query_ref.shape[2] // width
    factor = 1.0 / math.sqrt(HS)

    def remote(src, dst, send, recv, **where):
        return pltpu.make_async_remote_copy(
            src_ref=src, dst_ref=dst, send_sem=send, recv_sem=recv,
            device_id=where, device_id_type=MESH)

    def unless(cond, fn):
        pl.when(jnp.logical_not(cond))(fn)

    barrier = pltpu.get_barrier_semaphore()

    def greet(**where):
        pl.semaphore_signal(barrier, inc=1, device_id=where, device_id_type=MESH)

    for g2 in range(ng):
        for c in range(ratio):
            unless(diagonal & (g2 == g) & (c == piece),
                   lambda g2=g2, c=c: greet(glob=jnp.int32(g2), byte=g * ratio + c))
    for s in range(nb):
        unless(diagonal & (s == b), lambda s=s: greet(glob=owner, byte=jnp.int32(s)))
    for o in range(1, nb):
        greet(byte=lax.rem(b + o, nb))
    for o in range(1, ng):
        greet(glob=lax.rem(g + o, ng))
    for o in range(1, nd):
        greet(dp=lax.rem(dp + o, nd))
    fetch[0].wait()
    fetch[1].wait()

    row = start_ref[0, pl.ds(b, 1), :]
    i0 = lax.broadcasted_iota(jnp.int32, (slots, slots), 0)
    i1 = lax.broadcasted_iota(jnp.int32, (slots, slots), 1)
    spread = jnp.broadcast_to(row, (slots, slots))
    first = jnp.sum(jnp.where(i0 == i1, spread, 0), axis=1, keepdims=True)
    after = jnp.sum(jnp.where(i0 + 1 == i1, spread, 0), axis=1, keepdims=True)
    slot_col = lax.broadcasted_iota(jnp.int32, (slots, 1), 0)
    after = jnp.where(slot_col == slots - 1, byte_count, after)
    position = lax.broadcasted_iota(jnp.int32, (slots, byte_count), 1)
    members = jnp.where((first <= position) & (position < after), 1.0, 0.0).astype(F32)
    counts = jnp.maximum(jnp.sum(members, axis=1, keepdims=True), 1.0)
    members = members.astype(BF16)
    for c in range(ratio):
        summed = mm(members, states_ref[0, :, c * chunk:(c + 1) * chunk], 1, 0)
        means = (summed / counts).astype(BF16)
        for i in range(ng):
            pooled[c, i] = means[:, i * part:(i + 1) * part]

    pl.semaphore_wait(barrier, 2 * nb - 2 * jnp.where(diagonal, 1, 0) + nb - 1 + ng - 1 + nd - 1)

    def pool_copy(g2, c):
        return remote(pooled.at[c, g2], quarter.at[b], s1.at[g2 * ratio + c], r1.at[b],
                      glob=jnp.int32(g2), byte=g * ratio + c)

    for g2 in range(ng):
        for c in range(ratio):
            unless(diagonal & (g2 == g) & (c == piece), lambda g2=g2, c=c: pool_copy(g2, c).start())

    @pl.when(diagonal)
    def _():
        quarter[b] = pooled[piece, g]

    spots = lax.broadcasted_iota(jnp.int32, (slots, total), 1)
    tiles = jnp.where(lax.rem(spots, slots) == lax.broadcasted_iota(jnp.int32, (slots, total), 0), 1.0, 0.0)
    used = jnp.where(start_ref[0] < byte_count, 1.0, 0.0)
    used = mm(used.astype(BF16), tiles.astype(BF16), 1, 0)
    lane = lax.broadcasted_iota(jnp.int32, (nb, total), 1)
    shard_of = lax.broadcasted_iota(jnp.int32, (nb, total), 0)
    mine = (lane >= shard_of * slots) & (lane < (shard_of + 1) * slots)
    used = jnp.sum(jnp.where(mine, used, 0.0), axis=0, keepdims=True)
    live = jnp.where(first < byte_count, 1.0, 0.0)
    lives = jnp.concatenate([live] * group, axis=0)
    rows = group * slots
    ids = b * slots + lax.rem(lax.broadcasted_iota(jnp.int32, (rows, total), 0), slots)
    keys = lax.broadcasted_iota(jnp.int32, (rows, total), 1)
    visible = (keys <= ids) & (jnp.broadcast_to(used, (rows, total)) > 0.5)

    heads = []
    fetch[4].wait()
    fetch[5].wait()
    for c in range(shared):
        cols = [slice((c * group + h) * HS, (c * group + h + 1) * HS) for h in range(group)]
        q = jnp.concatenate([query_ref[0, :, at] for at in cols], axis=0)
        gm = jnp.concatenate([cot_ref[0, :, at] for at in cols], axis=0).astype(F32) * lives
        heads.append((cols, q, gm, gm.astype(BF16)))
    fetch[2].wait()
    fetch[3].wait()
    wt_ref[...] = w_ref[...].T

    for s in range(nb):
        unless(diagonal & (s == b), lambda s=s: remote(
            pooled.at[0, 0], quarter.at[s], s1.at[0], r1.at[s], byte=b).wait_recv())

    def plane_copy(o, slot):
        return remote(quarter, pool_all.at[dp, slot], s0.at[o], r0.at[slot], glob=lax.rem(g + o, ng))

    for o in range(1, ng):
        plane_copy(o, g).start()
    pool_all[dp, g] = quarter[...]
    for o in range(1, ng):
        plane_copy(o, lax.rem(g + o, ng)).wait_recv()

    for o in range(1, nd):
        remote(pool_all.at[dp], pool_all.at[dp], sd.at[0, o], rd.at[0, dp], dp=lax.rem(dp + o, nd)).start()

    acc = mm(pool_all[dp, 0].reshape(total, part), w_ref[:part], 1, 0)
    for i in range(1, ng):
        acc = acc + mm(pool_all[dp, i].reshape(total, part), w_ref[i * part:(i + 1) * part], 1, 0)
    kv_part[...] = acc.astype(BF16).reshape(nb, slots, 2 * width)

    def reduce(part, recv, whole, sa, ra, sb, rb, beside=None):
        for o in range(1, nb):
            peer = lax.rem(b + o, nb)
            remote(part.at[peer], recv.at[b], sa.at[o], ra.at[b], byte=peer).start()
        if beside is not None:
            beside()
        acc = part[b].astype(F32)
        for o in range(1, nb):
            peer = lax.rem(b + o, nb)
            remote(part.at[peer], recv.at[peer], sa.at[o], ra.at[peer], byte=peer).wait_recv()
            acc = acc + recv[peer].astype(F32)
        whole[b] = acc.astype(BF16)
        for o in range(1, nb):
            remote(whole.at[b], whole.at[b], sb.at[o], rb.at[b], byte=lax.rem(b + o, nb)).start()
        for o in range(1, nb):
            peer = lax.rem(b + o, nb)
            remote(whole.at[b], whole.at[peer], sb.at[o], rb.at[peer], byte=peer).wait_recv()

    def sent(part, whole, recv, sa, ra, sb, rb):
        for o in range(1, nb):
            peer = lax.rem(b + o, nb)
            remote(part.at[peer], recv.at[b], sa.at[o], ra.at[b], byte=peer).wait_send()
            remote(whole.at[b], whole.at[b], sb.at[o], rb.at[b], byte=peer).wait_send()

    reduce(kv_part, kv_recv, kv_all, s2, r2, s3, r3)

    done = []
    for c in range(shared):
        k = kv_all[:, :, c * HS:(c + 1) * HS].reshape(total, HS)
        v = kv_all[:, :, width + c * HS:width + (c + 1) * HS].reshape(total, HS)
        cols, q, gm, gm16 = heads[c]
        scores = jnp.where(visible, mm(q, k, 1, 1) * factor, -1e30)
        top = jnp.max(scores, axis=1, keepdims=True)
        raised = jnp.where(visible, jnp.exp(scores - top), 0.0)
        prob = raised / jnp.maximum(jnp.sum(raised, axis=1, keepdims=True), 1.0)
        pb = prob.astype(BF16)
        mixed = mm(pb, v, 1, 0)
        dots = jnp.sum(gm * mixed, axis=1, keepdims=True)
        ds = (prob * (mm(gm16, v, 1, 1) - dots) * factor).astype(BF16)
        dkv_part[:, :, c * HS:(c + 1) * HS] = mm(ds, q, 0, 0).astype(BF16).reshape(nb, slots, HS)
        dkv_part[:, :, width + c * HS:width + (c + 1) * HS] = (
            mm(pb, gm16, 0, 0).astype(BF16).reshape(nb, slots, HS))
        done.append((cols, mixed, ds, k))

    def outputs():
        for cols, mixed, ds, k in done:
            att = (mixed * lives).astype(BF16)
            gq = mm(ds, k, 1, 0).astype(BF16)
            for h in range(group):
                att_ref[0, :, cols[h]] = att[h * slots:(h + 1) * slots]
                gq_ref[0, :, cols[h]] = gq[h * slots:(h + 1) * slots]
        give[0].start()
        give[1].start()

    reduce(dkv_part, dkv_recv, dkv_all.at[dp], s4, r4, s5, r5, outputs)
    for o in range(1, nd):
        remote(dkv_all.at[dp], dkv_all.at[dp], sd.at[1, o], rd.at[1, dp], dp=lax.rem(dp + o, nd)).start()

    dkv = dkv_all[dp].reshape(total, 2 * width)
    terms = mm(dkv, wt_ref[...], 1, 0)
    for i in range(ng):
        dpart[i] = terms[:, i * part:(i + 1) * part].astype(BF16).reshape(nb, slots, part)

    def cut_copy(o, slot):
        peer = lax.rem(g + o, ng)
        return remote(dpart.at[peer], dterm.at[slot], s7.at[o], r7.at[slot], glob=peer)

    for o in range(1, ng):
        cut_copy(o, g).start()

    for o in range(1, nd):
        other = lax.rem(dp + o, nd)
        remote(pool_all.at[dp], pool_all.at[other], sd.at[0, o], rd.at[0, other], dp=other).wait_recv()
        remote(dkv_all.at[dp], dkv_all.at[other], sd.at[1, o], rd.at[1, other], dp=other).wait_recv()
    both = dkv_all[...].reshape(nd * total, 2 * width)
    def weights(i):
        product = mm(pool_all[:, i].reshape(nd * total, part), both, 0, 0)
        for j in range(2):
            gkv_ref[j, i * part:(i + 1) * part, :] = product[:, j * width:(j + 1) * width]

    for i in range(ng // 2):
        weights(i)

    acc = dpart[g].astype(F32)
    for o in range(1, ng):
        peer = lax.rem(g + o, ng)
        cut_copy(o, peer).wait_recv()
        acc = acc + dterm[peer].astype(F32)
    dsum[...] = acc.astype(BF16)

    def patch_copy(s):
        return remote(dsum.at[s], drecv.at[g, piece], s6.at[s], r6.at[g, piece], glob=owner, byte=jnp.int32(s))

    for s in range(nb):
        unless(diagonal & (s == b), lambda s=s: patch_copy(s).start())

    @pl.when(diagonal)
    def _():
        drecv[g, piece] = dsum[b]

    for i in range(ng // 2, ng):
        weights(i)
    give[3].start()

    for g2 in range(ng):
        for c in range(ratio):
            unless(diagonal & (g2 == g) & (c == piece), lambda g2=g2, c=c: remote(
                dsum.at[0], drecv.at[g2, c], s6.at[0], r6.at[g2, c], byte=b).wait_recv())
    for c in range(ratio):
        for i in range(ng):
            share = (drecv[i, c].astype(F32) / counts).astype(BF16)
            first_col = c * chunk + i * part
            gb_ref[0, :, first_col:first_col + part] = mm(members, share, 0, 0).astype(BF16)
    give[2].start()

    for g2 in range(ng):
        for c in range(ratio):
            unless(diagonal & (g2 == g) & (c == piece), lambda g2=g2, c=c: pool_copy(g2, c).wait_send())
    sent(kv_part, kv_all, kv_recv, s2, r2, s3, r3)
    sent(dkv_part, dkv_all.at[dp], dkv_recv, s4, r4, s5, r5)
    for o in range(1, ng):
        plane_copy(o, g).wait_send()
        cut_copy(o, g).wait_send()
    for s in range(nb):
        unless(diagonal & (s == b), lambda s=s: patch_copy(s).wait_send())
    for o in range(1, nd):
        other = lax.rem(dp + o, nd)
        remote(pool_all.at[dp], pool_all.at[dp], sd.at[0, o], rd.at[0, dp], dp=other).wait_send()
        remote(dkv_all.at[dp], dkv_all.at[dp], sd.at[1, o], rd.at[1, dp], dp=other).wait_send()
    for store in give:
        store.wait()


def hand_on(*refs):
    count = (len(refs) - 2) // 3
    given, taken, held = refs[:count], refs[count:2 * count], refs[2 * count:3 * count]
    loads, stores = refs[-2:]
    inward, outward = [], []
    for at in range(count):
        for lead in range(given[at].shape[0]):
            slot = len(inward)
            inward.append(pltpu.make_async_copy(given[at].at[lead], held[at].at[lead], loads.at[slot]))
            outward.append(pltpu.make_async_copy(held[at].at[lead], taken[at].at[lead], stores.at[slot]))
    for move in inward:
        move.start()
    for back, move in zip(inward, outward):
        back.wait()
        move.start()
    for move in outward:
        move.wait()


def on_device(nd, ng, nb, byte_states, patch_start, queries, grad_out, w_kv):
    slots = patch_start.shape[2]
    chunk, width = w_kv.shape[1], w_kv.shape[2]
    ratio = nb // ng
    part = chunk // ng
    dma = pltpu.SemaphoreType.DMA
    hbm = pl.BlockSpec(memory_space=pltpu.HBM)
    found = pl.pallas_call(
        functools.partial(kernel, nd, ng, nb),
        out_shape=(
            jax.ShapeDtypeStruct(queries.shape, BF16),
            jax.ShapeDtypeStruct(queries.shape, BF16),
            jax.ShapeDtypeStruct(byte_states.shape, BF16),
            jax.ShapeDtypeStruct(w_kv.shape, F32),
        ),
        in_specs=[hbm] * 5,
        out_specs=(hbm,) * 4,
        scratch_shapes=[
            pltpu.VMEM(byte_states.shape, BF16),
            pltpu.VMEM(patch_start.shape, patch_start.dtype),
            pltpu.VMEM(queries.shape, BF16),
            pltpu.VMEM(grad_out.shape, BF16),
            pltpu.VMEM((chunk, 2 * width), BF16),
            pltpu.VMEM((2 * width, chunk), BF16),
            dma((6,)),
            pltpu.VMEM(queries.shape, BF16),
            pltpu.VMEM(queries.shape, BF16),
            pltpu.VMEM(byte_states.shape, BF16),
            pltpu.VMEM(w_kv.shape, F32),
            dma((4,)),
            pltpu.VMEM((ratio, ng, slots, part), BF16),
            pltpu.VMEM((nb, slots, part), BF16),
            pltpu.VMEM((nd, ng, nb, slots, part), BF16),
            pltpu.VMEM((nb, slots, 2 * width), BF16),
            pltpu.VMEM((nb, slots, 2 * width), BF16),
            pltpu.VMEM((nb, slots, 2 * width), BF16),
            pltpu.VMEM((nb, slots, 2 * width), BF16),
            pltpu.VMEM((nb, slots, 2 * width), BF16),
            pltpu.VMEM((nd, nb, slots, 2 * width), BF16),
            pltpu.VMEM((ng, nb, slots, part), BF16),
            pltpu.VMEM((ng, nb, slots, part), BF16),
            pltpu.VMEM((nb, slots, part), BF16),
            pltpu.VMEM((ng, ratio, slots, part), BF16),
            dma((ng,)), dma((ng,)), dma((ng,)), dma((ng,)),
            dma((nb,)), dma((nb,)), dma((nb,)), dma((nb,)), dma((nb,)), dma((nb,)),
            dma((nb,)), dma((nb,)), dma((nb,)), dma((nb,)), dma((nb,)), dma((ng, ratio)),
            dma((2, nd)), dma((2, nd)),
        ],
        compiler_params=pltpu.CompilerParams(
            collective_id=0, has_side_effects=True, vmem_limit_bytes=56 * 1024 * 1024),
    )(byte_states, patch_start, queries, grad_out, w_kv)
    return pl.pallas_call(
        hand_on,
        out_shape=tuple(jax.ShapeDtypeStruct(one.shape, one.dtype) for one in found),
        in_specs=[pl.BlockSpec(memory_space=pl.ANY)] * 4,
        out_specs=(hbm,) * 4,
        scratch_shapes=[pltpu.VMEM(one.shape, one.dtype) for one in found]
        + [dma((sum(one.shape[0] for one in found),))] * 2,
    )(*found)


def solution(mesh):
    sizes = (mesh.shape["dp"], mesh.shape["glob"], mesh.shape["byte"])
    placed = (
        P("dp", "byte", "glob"),
        P("dp", None, None),
        P("dp", "byte", "glob"),
        P("dp", "byte", "glob"),
        P(None, "byte", "glob"),
    )
    return jax.shard_map(
        functools.partial(on_device, *sizes),
        mesh=mesh,
        in_specs=placed,
        out_specs=(
            P("dp", "byte", "glob"),
            P("dp", "byte", "glob"),
            P("dp", "byte", "glob"),
            P(None, "byte", "glob"),
        ),
        check_vma=False,
    )
```

```python
import functools
import math

import jax
import jax.numpy as jnp
from jax import lax
from jax.experimental import pallas as pl
from jax.experimental.pallas import tpu as pltpu
from jax.sharding import PartitionSpec as P

HS = 128
MESH = pl.DeviceIdType.MESH
F32 = jnp.float32
BF16 = jnp.bfloat16


def mm(left, right, a, b):
    return lax.dot_general(left, right, (((a,), (b,)), ((), ())), preferred_element_type=F32)


def kernel(nd, ng, nb, states_hbm, start_hbm, query_hbm, cot_hbm, w_hbm,
           att_hbm, gq_hbm, gb_hbm, gkv_hbm,
           states_ref, start_ref, query_ref, cot_ref, w_ref, wt_ref, loads,
           att_ref, gq_ref, gb_ref, gkv_ref, stores,
           pooled, quarter, pool_all, kv_part, kv_recv, kv_all, dkv_part, dkv_recv, dkv_all, dpart, dterm, dsum, drecv,
           s0, r0, s7, r7, s1, r1, s2, r2, s3, r3, s4, r4, s5, r5, s6, r6, sd, rd):
    fetch = [pltpu.make_async_copy(src, dst, loads.at[at]) for at, (src, dst) in enumerate((
        (start_hbm, start_ref), (states_hbm, states_ref),
        (w_hbm.at[0], w_ref.at[:, :w_hbm.shape[2]]), (w_hbm.at[1], w_ref.at[:, w_hbm.shape[2]:]),
        (query_hbm, query_ref), (cot_hbm, cot_ref)))]
    give = [pltpu.make_async_copy(src, dst, stores.at[at]) for at, (src, dst) in enumerate((
        (att_ref, att_hbm), (gq_ref, gq_hbm), (gb_ref, gb_hbm), (gkv_ref, gkv_hbm)))]
    for load in fetch:
        load.start()
    dp = lax.axis_index("dp")
    g = lax.axis_index("glob")
    b = lax.axis_index("byte")
    ratio = nb // ng
    owner = b // ratio
    piece = lax.rem(b, ratio)
    diagonal = g == owner
    byte_count = states_ref.shape[1]
    slots = start_ref.shape[2]
    total = nb * slots
    chunk = w_ref.shape[0]
    width = w_ref.shape[1] // 2
    shared = width // HS
    part = chunk // ng
    group = query_ref.shape[2] // width
    factor = 1.0 / math.sqrt(HS)

    def remote(src, dst, send, recv, **where):
        return pltpu.make_async_remote_copy(
            src_ref=src, dst_ref=dst, send_sem=send, recv_sem=recv,
            device_id=where, device_id_type=MESH)

    def unless(cond, fn):
        pl.when(jnp.logical_not(cond))(fn)

    barrier = pltpu.get_barrier_semaphore()

    def greet(**where):
        pl.semaphore_signal(barrier, inc=1, device_id=where, device_id_type=MESH)

    for g2 in range(ng):
        for c in range(ratio):
            unless(diagonal & (g2 == g) & (c == piece),
                   lambda g2=g2, c=c: greet(glob=jnp.int32(g2), byte=g * ratio + c))
    for s in range(nb):
        unless(diagonal & (s == b), lambda s=s: greet(glob=owner, byte=jnp.int32(s)))
    for o in range(1, nb):
        greet(byte=lax.rem(b + o, nb))
    for o in range(1, ng):
        greet(glob=lax.rem(g + o, ng))
    for o in range(1, nd):
        greet(dp=lax.rem(dp + o, nd))
    fetch[0].wait()
    fetch[1].wait()

    row = start_ref[0, pl.ds(b, 1), :]
    i0 = lax.broadcasted_iota(jnp.int32, (slots, slots), 0)
    i1 = lax.broadcasted_iota(jnp.int32, (slots, slots), 1)
    spread = jnp.broadcast_to(row, (slots, slots))
    first = jnp.sum(jnp.where(i0 == i1, spread, 0), axis=1, keepdims=True)
    after = jnp.sum(jnp.where(i0 + 1 == i1, spread, 0), axis=1, keepdims=True)
    slot_col = lax.broadcasted_iota(jnp.int32, (slots, 1), 0)
    after = jnp.where(slot_col == slots - 1, byte_count, after)
    position = lax.broadcasted_iota(jnp.int32, (slots, byte_count), 1)
    members = jnp.where((first <= position) & (position < after), 1.0, 0.0).astype(F32)
    counts = jnp.maximum(jnp.sum(members, axis=1, keepdims=True), 1.0)
    members = members.astype(BF16)
    for c in range(ratio):
        summed = mm(members, states_ref[0, :, c * chunk:(c + 1) * chunk], 1, 0)
        means = (summed / counts).astype(BF16)
        for i in range(ng):
            pooled[c, i] = means[:, i * part:(i + 1) * part]

    pl.semaphore_wait(barrier, 2 * nb - 2 * jnp.where(diagonal, 1, 0) + nb - 1 + ng - 1 + nd - 1)

    def pool_copy(g2, c):
        return remote(pooled.at[c, g2], quarter.at[b], s1.at[g2 * ratio + c], r1.at[b],
                      glob=jnp.int32(g2), byte=g * ratio + c)

    for g2 in range(ng):
        for c in range(ratio):
            unless(diagonal & (g2 == g) & (c == piece), lambda g2=g2, c=c: pool_copy(g2, c).start())

    @pl.when(diagonal)
    def _():
        quarter[b] = pooled[piece, g]

    spots = lax.broadcasted_iota(jnp.int32, (slots, total), 1)
    tiles = jnp.where(lax.rem(spots, slots) == lax.broadcasted_iota(jnp.int32, (slots, total), 0), 1.0, 0.0)
    used = jnp.where(start_ref[0] < byte_count, 1.0, 0.0)
    used = mm(used.astype(BF16), tiles.astype(BF16), 1, 0)
    lane = lax.broadcasted_iota(jnp.int32, (nb, total), 1)
    shard_of = lax.broadcasted_iota(jnp.int32, (nb, total), 0)
    mine = (lane >= shard_of * slots) & (lane < (shard_of + 1) * slots)
    used = jnp.sum(jnp.where(mine, used, 0.0), axis=0, keepdims=True)
    live = jnp.where(first < byte_count, 1.0, 0.0)
    lives = jnp.concatenate([live] * group, axis=0)
    rows = group * slots
    ids = b * slots + lax.rem(lax.broadcasted_iota(jnp.int32, (rows, total), 0), slots)
    keys = lax.broadcasted_iota(jnp.int32, (rows, total), 1)
    visible = (keys <= ids) & (jnp.broadcast_to(used, (rows, total)) > 0.5)

    heads = []
    fetch[4].wait()
    fetch[5].wait()
    for c in range(shared):
        cols = [slice((c * group + h) * HS, (c * group + h + 1) * HS) for h in range(group)]
        q = jnp.concatenate([query_ref[0, :, at] for at in cols], axis=0)
        gm = jnp.concatenate([cot_ref[0, :, at] for at in cols], axis=0).astype(F32) * lives
        heads.append((cols, q, gm, gm.astype(BF16)))
    fetch[2].wait()
    fetch[3].wait()
    wt_ref[...] = w_ref[...].T

    def plane_copy(o, slot, s):
        return remote(quarter.at[s], pool_all.at[dp, slot, s], s0.at[o, s], r0.at[slot, s],
                      glob=lax.rem(g + o, ng))

    for k in range(nb):
        s = lax.rem(b + k, nb)

        def arrive(s=s):
            remote(pooled.at[0, 0], quarter.at[s], s1.at[0], r1.at[s], byte=b).wait_recv()

        unless(diagonal, arrive) if k == 0 else arrive()
        for o in range(1, ng):
            plane_copy(o, g, s).start()
    pool_all[dp, g] = quarter[...]
    for k in range(nb):
        for o in range(1, ng):
            plane_copy(o, lax.rem(g + o, ng), lax.rem(b + k, nb)).wait_recv()

    for o in range(1, nd):
        remote(pool_all.at[dp], pool_all.at[dp], sd.at[0, o], rd.at[0, dp], dp=lax.rem(dp + o, nd)).start()

    acc = mm(pool_all[dp, 0].reshape(total, part), w_ref[:part], 1, 0)
    for i in range(1, ng):
        acc = acc + mm(pool_all[dp, i].reshape(total, part), w_ref[i * part:(i + 1) * part], 1, 0)
    kv_part[...] = acc.astype(BF16).reshape(nb, slots, 2 * width)

    def reduce(part, recv, whole, sa, ra, sb, rb, beside=None):
        for o in range(1, nb):
            peer = lax.rem(b + o, nb)
            remote(part.at[peer], recv.at[b], sa.at[o], ra.at[b], byte=peer).start()
        if beside is not None:
            beside()
        acc = part[b].astype(F32)
        for o in range(1, nb):
            peer = lax.rem(b + o, nb)
            remote(part.at[peer], recv.at[peer], sa.at[o], ra.at[peer], byte=peer).wait_recv()
            acc = acc + recv[peer].astype(F32)
        whole[b] = acc.astype(BF16)
        for o in range(1, nb):
            remote(whole.at[b], whole.at[b], sb.at[o], rb.at[b], byte=lax.rem(b + o, nb)).start()
        for o in range(1, nb):
            peer = lax.rem(b + o, nb)
            remote(whole.at[b], whole.at[peer], sb.at[o], rb.at[peer], byte=peer).wait_recv()

    def sent(part, whole, recv, sa, ra, sb, rb):
        for o in range(1, nb):
            peer = lax.rem(b + o, nb)
            remote(part.at[peer], recv.at[b], sa.at[o], ra.at[b], byte=peer).wait_send()
            remote(whole.at[b], whole.at[b], sb.at[o], rb.at[b], byte=peer).wait_send()

    reduce(kv_part, kv_recv, kv_all, s2, r2, s3, r3)

    done = []
    for c in range(shared):
        k = kv_all[:, :, c * HS:(c + 1) * HS].reshape(total, HS)
        v = kv_all[:, :, width + c * HS:width + (c + 1) * HS].reshape(total, HS)
        cols, q, gm, gm16 = heads[c]
        scores = jnp.where(visible, mm(q, k, 1, 1) * factor, -1e30)
        top = jnp.max(scores, axis=1, keepdims=True)
        raised = jnp.where(visible, jnp.exp(scores - top), 0.0)
        prob = raised / jnp.maximum(jnp.sum(raised, axis=1, keepdims=True), 1.0)
        pb = prob.astype(BF16)
        mixed = mm(pb, v, 1, 0)
        dots = jnp.sum(gm * mixed, axis=1, keepdims=True)
        ds = (prob * (mm(gm16, v, 1, 1) - dots) * factor).astype(BF16)
        dkv_part[:, :, c * HS:(c + 1) * HS] = mm(ds, q, 0, 0).astype(BF16).reshape(nb, slots, HS)
        dkv_part[:, :, width + c * HS:width + (c + 1) * HS] = (
            mm(pb, gm16, 0, 0).astype(BF16).reshape(nb, slots, HS))
        done.append((cols, mixed, ds, k))

    def outputs():
        for cols, mixed, ds, k in done:
            att = (mixed * lives).astype(BF16)
            gq = mm(ds, k, 1, 0).astype(BF16)
            for h in range(group):
                att_ref[0, :, cols[h]] = att[h * slots:(h + 1) * slots]
                gq_ref[0, :, cols[h]] = gq[h * slots:(h + 1) * slots]
        give[0].start()
        give[1].start()

    reduce(dkv_part, dkv_recv, dkv_all.at[dp], s4, r4, s5, r5, outputs)
    for o in range(1, nd):
        remote(dkv_all.at[dp], dkv_all.at[dp], sd.at[1, o], rd.at[1, dp], dp=lax.rem(dp + o, nd)).start()

    dkv = dkv_all[dp].reshape(total, 2 * width)
    terms = mm(dkv, wt_ref[...], 1, 0)
    for i in range(ng):
        dpart[i] = terms[:, i * part:(i + 1) * part].astype(BF16).reshape(nb, slots, part)

    def cut_copy(o, slot, s):
        peer = lax.rem(g + o, ng)
        return remote(dpart.at[peer, s], dterm.at[slot, s], s7.at[o, s], r7.at[slot, s], glob=peer)

    for k in range(nb):
        for o in range(1, ng):
            cut_copy(o, g, lax.rem(b + k + 1, nb)).start()

    for o in range(1, nd):
        other = lax.rem(dp + o, nd)
        remote(pool_all.at[dp], pool_all.at[other], sd.at[0, o], rd.at[0, other], dp=other).wait_recv()
        remote(dkv_all.at[dp], dkv_all.at[other], sd.at[1, o], rd.at[1, other], dp=other).wait_recv()
    both = dkv_all[...].reshape(nd * total, 2 * width)
    def weights(i):
        product = mm(pool_all[:, i].reshape(nd * total, part), both, 0, 0)
        for j in range(2):
            gkv_ref[j, i * part:(i + 1) * part, :] = product[:, j * width:(j + 1) * width]

    for i in range(ng // 2):
        weights(i)

    def patch_copy(s):
        return remote(dsum.at[s], drecv.at[g, piece], s6.at[s], r6.at[g, piece], glob=owner, byte=s)

    for k in range(nb):
        s = lax.rem(b + k + 1, nb)
        acc = dpart[g, s].astype(F32)
        for o in range(1, ng):
            peer = lax.rem(g + o, ng)
            cut_copy(o, peer, s).wait_recv()
            acc = acc + dterm[peer, s].astype(F32)
        dsum[s] = acc.astype(BF16)
        if k < nb - 1:
            patch_copy(s).start()
        else:
            unless(diagonal, lambda s=s: patch_copy(s).start())

    @pl.when(diagonal)
    def _():
        drecv[g, piece] = dsum[b]

    for i in range(ng // 2, ng):
        weights(i)
    give[3].start()

    for g2 in range(ng):
        for c in range(ratio):
            unless(diagonal & (g2 == g) & (c == piece), lambda g2=g2, c=c: remote(
                dsum.at[0], drecv.at[g2, c], s6.at[0], r6.at[g2, c], byte=b).wait_recv())
    for c in range(ratio):
        for i in range(ng):
            share = (drecv[i, c].astype(F32) / counts).astype(BF16)
            first_col = c * chunk + i * part
            gb_ref[0, :, first_col:first_col + part] = mm(members, share, 0, 0).astype(BF16)
    give[2].start()

    for g2 in range(ng):
        for c in range(ratio):
            unless(diagonal & (g2 == g) & (c == piece), lambda g2=g2, c=c: pool_copy(g2, c).wait_send())
    sent(kv_part, kv_all, kv_recv, s2, r2, s3, r3)
    sent(dkv_part, dkv_all.at[dp], dkv_recv, s4, r4, s5, r5)
    for o in range(1, ng):
        for s in range(nb):
            plane_copy(o, g, s).wait_send()
            cut_copy(o, g, s).wait_send()
    for s in range(nb):
        unless(diagonal & (s == b), lambda s=s: patch_copy(jnp.int32(s)).wait_send())
    for o in range(1, nd):
        other = lax.rem(dp + o, nd)
        remote(pool_all.at[dp], pool_all.at[dp], sd.at[0, o], rd.at[0, dp], dp=other).wait_send()
        remote(dkv_all.at[dp], dkv_all.at[dp], sd.at[1, o], rd.at[1, dp], dp=other).wait_send()
    for store in give:
        store.wait()


def hand_on(*refs):
    count = (len(refs) - 2) // 3
    given, taken, held = refs[:count], refs[count:2 * count], refs[2 * count:3 * count]
    loads, stores = refs[-2:]
    inward, outward = [], []
    for at in range(count):
        for lead in range(given[at].shape[0]):
            slot = len(inward)
            inward.append(pltpu.make_async_copy(given[at].at[lead], held[at].at[lead], loads.at[slot]))
            outward.append(pltpu.make_async_copy(held[at].at[lead], taken[at].at[lead], stores.at[slot]))
    for move in inward:
        move.start()
    for back, move in zip(inward, outward):
        back.wait()
        move.start()
    for move in outward:
        move.wait()


def on_device(nd, ng, nb, byte_states, patch_start, queries, grad_out, w_kv):
    slots = patch_start.shape[2]
    chunk, width = w_kv.shape[1], w_kv.shape[2]
    ratio = nb // ng
    part = chunk // ng
    dma = pltpu.SemaphoreType.DMA
    hbm = pl.BlockSpec(memory_space=pltpu.HBM)
    found = pl.pallas_call(
        functools.partial(kernel, nd, ng, nb),
        out_shape=(
            jax.ShapeDtypeStruct(queries.shape, BF16),
            jax.ShapeDtypeStruct(queries.shape, BF16),
            jax.ShapeDtypeStruct(byte_states.shape, BF16),
            jax.ShapeDtypeStruct(w_kv.shape, F32),
        ),
        in_specs=[hbm] * 5,
        out_specs=(hbm,) * 4,
        scratch_shapes=[
            pltpu.VMEM(byte_states.shape, BF16),
            pltpu.VMEM(patch_start.shape, patch_start.dtype),
            pltpu.VMEM(queries.shape, BF16),
            pltpu.VMEM(grad_out.shape, BF16),
            pltpu.VMEM((chunk, 2 * width), BF16),
            pltpu.VMEM((2 * width, chunk), BF16),
            dma((6,)),
            pltpu.VMEM(queries.shape, BF16),
            pltpu.VMEM(queries.shape, BF16),
            pltpu.VMEM(byte_states.shape, BF16),
            pltpu.VMEM(w_kv.shape, F32),
            dma((4,)),
            pltpu.VMEM((ratio, ng, slots, part), BF16),
            pltpu.VMEM((nb, slots, part), BF16),
            pltpu.VMEM((nd, ng, nb, slots, part), BF16),
            pltpu.VMEM((nb, slots, 2 * width), BF16),
            pltpu.VMEM((nb, slots, 2 * width), BF16),
            pltpu.VMEM((nb, slots, 2 * width), BF16),
            pltpu.VMEM((nb, slots, 2 * width), BF16),
            pltpu.VMEM((nb, slots, 2 * width), BF16),
            pltpu.VMEM((nd, nb, slots, 2 * width), BF16),
            pltpu.VMEM((ng, nb, slots, part), BF16),
            pltpu.VMEM((ng, nb, slots, part), BF16),
            pltpu.VMEM((nb, slots, part), BF16),
            pltpu.VMEM((ng, ratio, slots, part), BF16),
            dma((ng, nb)), dma((ng, nb)), dma((ng, nb)), dma((ng, nb)),
            dma((nb,)), dma((nb,)), dma((nb,)), dma((nb,)), dma((nb,)), dma((nb,)),
            dma((nb,)), dma((nb,)), dma((nb,)), dma((nb,)), dma((nb,)), dma((ng, ratio)),
            dma((2, nd)), dma((2, nd)),
        ],
        compiler_params=pltpu.CompilerParams(
            collective_id=0, has_side_effects=True, vmem_limit_bytes=56 * 1024 * 1024),
    )(byte_states, patch_start, queries, grad_out, w_kv)
    return pl.pallas_call(
        hand_on,
        out_shape=tuple(jax.ShapeDtypeStruct(one.shape, one.dtype) for one in found),
        in_specs=[pl.BlockSpec(memory_space=pl.ANY)] * 4,
        out_specs=(hbm,) * 4,
        scratch_shapes=[pltpu.VMEM(one.shape, one.dtype) for one in found]
        + [dma((sum(one.shape[0] for one in found),))] * 2,
    )(*found)


def solution(mesh):
    sizes = (mesh.shape["dp"], mesh.shape["glob"], mesh.shape["byte"])
    placed = (
        P("dp", "byte", "glob"),
        P("dp", None, None),
        P("dp", "byte", "glob"),
        P("dp", "byte", "glob"),
        P(None, "byte", "glob"),
    )
    return jax.shard_map(
        functools.partial(on_device, *sizes),
        mesh=mesh,
        in_specs=placed,
        out_specs=(
            P("dp", "byte", "glob"),
            P("dp", "byte", "glob"),
            P("dp", "byte", "glob"),
            P(None, "byte", "glob"),
        ),
        check_vma=False,
    )
```
